32 devices in a mesh: col: 4 (over z), dp: 8 (over y, x, core).
Axes of the slice: x: 2, y: 2, z: 4, core: 2. Of those that a mesh axis runs over, the one named last changes fastest.
Arguments:
- stem_map: bfloat16 [48, 16, 16, 256], P('dp'), may hold values from -6 to 6
- last_one: float32 [48, 16, 16, 256], P('dp'), may hold values from -6 to 6
- last_two: float32 [48, 8, 8, 512], P('dp'), may hold values from -6 to 6
- teach_one: bfloat16 [48, 16, 16, 256], P('dp'), may hold values from -6 to 6
- teach_two: bfloat16 [48, 8, 8, 512], P('dp'), may hold values from -6 to 6
- teacher_slot: int32 [48], P('dp'), may hold values from 0 to 5, as said below
- depth_one: bfloat16 [4, 49, 256], P('col'), may hold values from -0.875 to 0.875
- gains_one: float32 [4, 3, 256], P('col'), may hold values from 0.75 to 1.25
- inner_one: bfloat16 [4, 256, 1024], P('col'), may hold values from -0.375 to 0.375
- outer_one: bfloat16 [4, 1024, 256], P('col'), may hold values from -0.1875 to 0.1875
- depth_two: bfloat16 [4, 49, 512], P('col'), may hold values from -0.875 to 0.875
- gains_two: float32 [4, 3, 512], P('col'), may hold values from 0.75 to 1.25
- inner_two: bfloat16 [4, 512, 2048], P('col'), may hold values from -0.25 to 0.25
- outer_two: bfloat16 [4, 2048, 512], P('col'), may hold values from -0.125 to 0.125
- down_proj: bfloat16 [4, 1024, 512], P('col'), may hold values from -0.1875 to 0.1875
- up_proj: bfloat16 [4, 512, 256], P('col'), may hold values from -0.25 to 0.25
Outputs:
- grad_depth_one: float32 [4, 49, 256], P('col')
- grad_gains_one: float32 [4, 3, 256], P('col')
- grad_inner_one: float32 [4, 256, 1024], P('col')
- grad_outer_one: float32 [4, 1024, 256], P('col')
- grad_depth_two: float32 [4, 49, 512], P('col')
- grad_gains_two: float32 [4, 2, 512], P('col')
- grad_rev_two: float32 [4, 512], P('col')
- grad_inner_two: float32 [4, 512, 2048], P('col')
- grad_outer_two: float32 [4, 2048, 512], P('col')
- grad_down: float32 [4, 1024, 512], P('col')
- grad_up: float32 [4, 512, 256], P('col')
- stem_grad: float32 [48, 16, 16, 256], P('dp')
The draws below stay inside these ranges and needn't reach their ends.
Inputs may be any that keep to these rules, and one draw needn't show every extreme that they name: `teacher_slot`: each aligned block of 6 entries (the pages of one device) is a permutation of 0 to 5.
All inputs are finite; a program needn't handle non-finite values.
Results may differ from the reference program's by a relative error of at most 0.02.
Values sent between devices are 32-bit elements; how exact they have to be, the bound alone decides.
No kernel may reach another device: no remote copies, remote signals or barrier semaphores. Data moves between devices by JAX's collectives and lax.ppermute only.
A program may use at most 128 MiB of HBM per device.

```python
import jax
import jax.numpy as jnp
from jax import lax

C1 = 256
C2 = 512
EXPAND = 4
SIDE = 16
PAGES_DEV = 6
PAGES = 48
COLS = 4


def draw_teacher_slot(key, part):
    key = jax.random.fold_in(key, 11)
    block_keys = jax.random.split(key, PAGES // PAGES_DEV)
    blocks = jax.vmap(lambda single: jax.random.permutation(single, PAGES_DEV))(block_keys)
    return blocks.reshape(PAGES).astype(jnp.int32)


def block_levels(key, dims, cuts, least, high):
    def one(position, blocks):
        heights = jax.random.uniform(jax.random.fold_in(jax.random.fold_in(key, 6), position), (blocks,), jnp.float32, least / len(cuts), high / len(cuts))
        return jnp.repeat(jnp.exp(heights), dims[position] // blocks).reshape((-1,) + (1,) * (len(dims) - position - 1))

    factor_of = one(*cuts[0])
    for cut in cuts[1:]:
        factor_of = factor_of * one(*cut)
    return factor_of


def centred(key, extent, width, bound, pieces=(), dtype=jnp.bfloat16):
    level = block_levels(key, extent, pieces, -0.22, 0.18) if pieces else 1.0
    result = jax.random.normal(key, extent, jnp.float32) * width * level
    return jnp.minimum(jnp.maximum(result, -bound), bound).astype(dtype)


def setup_inputs(seed: int = 0) -> dict:
    seeds = jax.random.split(jax.random.key(seed), 17)
    stem_map = centred(seeds[0], (PAGES, SIDE, SIDE, C1), 1.0, 6.0, ((0, 8),))
    last_one = centred(seeds[1], (PAGES, SIDE, SIDE, C1), 1.0, 6.0, ((0, 8),), jnp.float32)
    last_two = centred(seeds[2], (PAGES, SIDE // 2, SIDE // 2, C2), 1.0, 6.0, ((0, 8),), jnp.float32)
    teach_one = centred(seeds[3], (PAGES, SIDE, SIDE, C1), 1.0, 6.0, ((0, 8),))
    teach_two = centred(seeds[4], (PAGES, SIDE // 2, SIDE // 2, C2), 1.0, 6.0, ((0, 8),))
    teacher_slot = draw_teacher_slot(jax.random.fold_in(seeds[16], 71), 0)
    depth_one = centred(seeds[6], (COLS, 49, C1), 49 ** -0.5, 0.875, ((0, 4),))
    gains_one = jnp.clip(1.0 + 0.05 * jax.random.normal(seeds[7], (COLS, 3, C1), jnp.float32), 0.75, 1.25)
    inner_one = centred(seeds[8], (COLS, C1, EXPAND * C1), C1 ** -0.5, 0.375, ((0, 4),))
    outer_one = centred(seeds[9], (COLS, EXPAND * C1, C1), (EXPAND * C1) ** -0.5, 0.1875, ((0, 4),))
    depth_two = centred(seeds[10], (COLS, 49, C2), 49 ** -0.5, 0.875, ((0, 4),))
    gains_two = jnp.clip(1.0 + 0.05 * jax.random.normal(seeds[11], (COLS, 3, C2), jnp.float32), 0.75, 1.25)
    inner_two = centred(seeds[12], (COLS, C2, EXPAND * C2), C2 ** -0.5, 0.25, ((0, 4),))
    outer_two = centred(seeds[13], (COLS, EXPAND * C2, C2), (EXPAND * C2) ** -0.5, 0.125, ((0, 4),))
    down_proj = centred(seeds[14], (COLS, 4 * C1, C2), (4 * C1) ** -0.5, 0.1875, ((0, 4),))
    up_proj = centred(seeds[15], (COLS, C2, C1), C2 ** -0.5, 0.25, ((0, 4),))
    return dict(stem_map=stem_map, last_one=last_one, last_two=last_two, teach_one=teach_one, teach_two=teach_two, teacher_slot=teacher_slot, depth_one=depth_one, gains_one=gains_one, inner_one=inner_one, outer_one=outer_one, depth_two=depth_two, gains_two=gains_two, inner_two=inner_two, outer_two=outer_two, down_proj=down_proj, up_proj=up_proj)


def depthwise(field_in, kernel_taps):
    side_cells = field_in.shape[1]
    padded = jnp.pad(field_in, ((0, 0), (3, 3), (3, 3), (0, 0)))
    running = jnp.zeros(field_in.shape, jnp.float32)
    for row_offset in range(7):
        for col_offset in range(7):
            running = running + padded[:, row_offset:row_offset + side_cells, col_offset:col_offset + side_cells, :] * kernel_taps[7 * row_offset + col_offset]
    return running

def norm_part(field_in, kernel_taps, gain_row):
    hidden = depthwise(field_in, kernel_taps)
    center = hidden - lax.optimization_barrier(jnp.mean(hidden, axis=-1, keepdims=True))
    spread = lax.optimization_barrier(jnp.mean(center * center, axis=-1, keepdims=True))
    return center * lax.rsqrt(spread + 1e-06) * gain_row

def patchify(field_in):
    page_count, side_cells, _, channels = field_in.shape
    half_side = side_cells // 2
    shaped = field_in.reshape(page_count, half_side, 2, half_side, 2, channels)
    return shaped.transpose(0, 1, 3, 2, 4, 5).reshape(page_count, half_side, half_side, 4 * channels)

def unpatch(field_in):
    page_count, half_side, _, width_all = field_in.shape
    channels = width_all // 4
    shaped = field_in.reshape(page_count, half_side, half_side, 2, 2, channels)
    return shaped.transpose(0, 1, 3, 2, 4, 5).reshape(page_count, 2 * half_side, 2 * half_side, channels)

def doubled(field_in):
    return jnp.repeat(jnp.repeat(field_in, 2, axis=1), 2, axis=2)

def pooled(field_in):
    page_count, side_cells, _, channels = field_in.shape
    shaped = field_in.reshape(page_count, side_cells // 2, 2, side_cells // 2, 2, channels)
    return lax.optimization_barrier(jnp.sum(shaped, axis=(2, 4)))

def contract(left_side, right_side):
    left_flat = left_side.reshape(-1, left_side.shape[-1])
    right_flat = right_side.reshape(-1, right_side.shape[-1])
    return lax.dot_general(left_flat, right_flat, (((0,), (0,)), ((), ())), preferred_element_type=jnp.float32)

def block_forward(field_in, depth, gains, inner, outer):
    normed = norm_part(field_in, depth.astype(jnp.float32), gains[0]).astype(jnp.bfloat16)
    pre_act = jnp.dot(normed, inner, preferred_element_type=jnp.float32)
    activation = jax.nn.gelu(pre_act).astype(jnp.bfloat16)
    block_out = jnp.dot(activation, outer, preferred_element_type=jnp.float32)
    return (gains[1] * block_out, (normed, pre_act, activation, block_out))

def block_backward(field_in, depth, gains, inner, outer, saved, grad_rise):
    normed, pre_act, activation, block_out = saved
    scale_grad = lax.optimization_barrier(jnp.sum(grad_rise * block_out, axis=(0, 1, 2)))
    grad_out = (grad_rise * gains[1]).astype(jnp.bfloat16)
    outer_grad = contract(activation, grad_out)
    grad_act = jnp.dot(grad_out, outer.T, preferred_element_type=jnp.float32)
    _, gelu_back = jax.vjp(jax.nn.gelu, pre_act)
    grad_pre = gelu_back(grad_act)[0].astype(jnp.bfloat16)
    inner_grad = contract(normed, grad_pre)
    grad_norm = jnp.dot(grad_pre, inner.T, preferred_element_type=jnp.float32)
    _, norm_back = jax.vjp(norm_part, field_in, depth.astype(jnp.float32), gains[0])
    field_grad, depth_grad, gain_grad = norm_back(grad_norm)
    return (field_grad, depth_grad, gain_grad, scale_grad, inner_grad, outer_grad)

def column_back(stem_part, high_one, high_two, grad_one, grad_two, weights):
    depth_one, gains_one, inner_one, outer_one, depth_two, gains_two, inner_two, outer_two, down_proj, up_proj = weights
    patches = patchify(high_one).astype(jnp.bfloat16)
    lowered = jnp.dot(patches, down_proj, preferred_element_type=jnp.float32)
    rise_two, saved_two = block_forward(lowered, depth_two, gains_two, inner_two, outer_two)
    prev_two = (high_two - rise_two) / gains_two[2]
    coarse = prev_two.astype(jnp.bfloat16)
    entry_field = stem_part.astype(jnp.float32) + doubled(jnp.dot(coarse, up_proj, preferred_element_type=jnp.float32))
    rise_one, saved_one = block_forward(entry_field, depth_one, gains_one, inner_one, outer_one)
    prev_one = (high_one - rise_one) / gains_one[2]
    gamma_two = lax.optimization_barrier(jnp.sum(grad_two * prev_two, axis=(0, 1, 2)))
    grad_low, depth_two_g, norm_two_g, scale_two_g, inner_two_g, outer_two_g = block_backward(lowered, depth_two, gains_two, inner_two, outer_two, saved_two, grad_two)
    low_rounded = grad_low.astype(jnp.bfloat16)
    down_grad = contract(patches, low_rounded)
    total_one = grad_one + unpatch(jnp.dot(low_rounded, down_proj.T, preferred_element_type=jnp.float32))
    gamma_one = lax.optimization_barrier(jnp.sum(total_one * prev_one, axis=(0, 1, 2)))
    grad_entry, depth_one_g, norm_one_g, scale_one_g, inner_one_g, outer_one_g = block_backward(entry_field, depth_one, gains_one, inner_one, outer_one, saved_one, total_one)
    pool_rounded = pooled(grad_entry).astype(jnp.bfloat16)
    up_grad = contract(coarse, pool_rounded)
    next_two = gains_two[2] * grad_two + jnp.dot(pool_rounded, up_proj.T, preferred_element_type=jnp.float32)
    next_one = gains_one[2] * total_one
    gradients = (depth_one_g, jnp.stack([norm_one_g, scale_one_g, gamma_one]), inner_one_g, outer_one_g, depth_two_g, jnp.stack([norm_two_g, scale_two_g, gamma_two]), inner_two_g, outer_two_g, down_grad, up_grad)
    return ((prev_one, prev_two, next_one, next_two), grad_entry, gradients)

def reference(stem_map, last_one, last_two, teach_one, teach_two, teacher_slot, depth_one, gains_one, inner_one, outer_one, depth_two, gains_two, inner_two, outer_two, down_proj, up_proj):
    offsets = (jnp.arange(PAGES) // PAGES_DEV * PAGES_DEV).astype(jnp.int32)
    source_rows = offsets + teacher_slot.astype(jnp.int32)
    target_one = teach_one[source_rows].astype(jnp.float32)
    target_two = teach_two[source_rows].astype(jnp.float32)
    carried = (last_one, last_two, (last_one - target_one) / SIDE, (last_two - target_two) / (SIDE // 2))
    stem_total = jnp.zeros(stem_map.shape, jnp.float32)
    arrays = (depth_one, gains_one, inner_one, outer_one, depth_two, gains_two, inner_two, outer_two, down_proj, up_proj)
    collected = []
    for column in range(COLS - 1, -1, -1):
        carried, entry_grad, gradients = column_back(stem_map, carried[0], carried[1], carried[2], carried[3], tuple((w[column] for w in arrays)))
        stem_total = stem_total + entry_grad
        collected.insert(0, gradients)
    stacked = [jnp.stack([g[k] for g in collected]) for k in range(10)]
    return (stacked[0], stacked[1], stacked[2], stacked[3], stacked[4], stacked[5][:, :2], stacked[5][:, 2], stacked[6], stacked[7], stacked[8], stacked[9], stem_total)
```

```python
import jax
import jax.numpy as jnp
from jax import lax
from jax.experimental import pallas as pl
from jax.experimental.pallas import tpu as pltpu
from jax.sharding import PartitionSpec as P

F32 = jnp.float32
BF16 = jnp.bfloat16
LANES = 128
EPS = 1e-06
G0 = 0.7978845608028654
G1 = 0.044715
NT = (((1,), (1,)), ((), ()))


def shift_rows(block, step):
    if step == 0:
        return block
    rolled = pltpu.roll(block, (-step) % 8, 0)
    place = lax.broadcasted_iota(jnp.int32, block.shape, 0) + step
    return jnp.where((place >= 0) & (place < 8), rolled, 0.0)


def fine_shifts(col_parity):
    return (-1, 0, 1, 2) if col_parity == 0 else (-2, -1, 0, 1)


def fill_fine(shifted, value, phase):
    for row in range(8):
        line = value[8 * row : 8 * row + 8]
        for k, step in enumerate(fine_shifts(phase & 1)):
            shifted[k, phase, 8 * row : 8 * row + 8, :] = shift_rows(line, step)


def fill_coarse(shifted, value):
    for row in range(8):
        line = value[8 * row : 8 * row + 8]
        for k in range(7):
            shifted[k, 8 * row : 8 * row + 8, :] = shift_rows(line, k - 3)


def fine_source(dj, b):
    off = dj + b - 3
    pj = off & 1
    step = (off - pj) // 2
    return pj, step + (1 if pj == 0 else 2)


def conv_fine(shifted, taps, out, flip):
    def lane_block(lb, carry):
        lanes = pl.ds(pl.multiple_of(lb * LANES, LANES), LANES)
        for dj in range(2):
            acc = [None] * 16
            for b in range(7):
                pj, k = fine_source(dj, b)
                w = []
                for a in range(7):
                    t = 48 - (7 * a + b) if flip else 7 * a + b
                    w.append(jnp.broadcast_to(taps[t : t + 1, lanes], (8, LANES)))
                for ip in range(16):
                    r = 8 * (ip >> 1)
                    x = shifted[k, 2 * (ip & 1) + pj, r : r + 8, lanes]
                    for a in range(7):
                        i = ip - (a - 3)
                        if 0 <= i < 16:
                            acc[i] = x * w[a] if acc[i] is None else acc[i] + x * w[a]
            for i in range(16):
                r = 8 * (i >> 1)
                out[2 * (i & 1) + dj, r : r + 8, lanes] = acc[i]
        return carry

    lax.fori_loop(0, shifted.shape[-1] // LANES, lane_block, 0)


def taps_fine(shifted, field, out):
    def lane_block(lb, carry):
        lanes = pl.ds(pl.multiple_of(lb * LANES, LANES), LANES)
        for b in range(7):
            acc = [None] * 7
            for dj in range(2):
                pj, k = fine_source(dj, b)
                v = [
                    field[2 * (i & 1) + dj, 8 * (i >> 1) : 8 * (i >> 1) + 8, lanes]
                    for i in range(16)
                ]
                for ip in range(16):
                    r = 8 * (ip >> 1)
                    x = shifted[k, 2 * (ip & 1) + pj, r : r + 8, lanes]
                    for a in range(7):
                        i = ip - (a - 3)
                        if 0 <= i < 16:
                            acc[a] = x * v[i] if acc[a] is None else acc[a] + x * v[i]
            for a in range(7):
                t = 48 - (7 * a + b)
                out[t : t + 1, lanes] = jnp.sum(acc[a], axis=0, keepdims=True)
        return carry

    lax.fori_loop(0, shifted.shape[-1] // LANES, lane_block, 0)


def conv_coarse(shifted, taps, out, flip):
    def lane_block(lb, carry):
        lanes = pl.ds(pl.multiple_of(lb * LANES, LANES), LANES)
        acc = [None] * 8
        for b in range(7):
            w = []
            for a in range(7):
                t = 48 - (7 * a + b) if flip else 7 * a + b
                w.append(jnp.broadcast_to(taps[t : t + 1, lanes], (8, LANES)))
            for ip in range(8):
                x = shifted[b, 8 * ip : 8 * ip + 8, lanes]
                for a in range(7):
                    i = ip - (a - 3)
                    if 0 <= i < 8:
                        acc[i] = x * w[a] if acc[i] is None else acc[i] + x * w[a]
        for i in range(8):
            out[8 * i : 8 * i + 8, lanes] = acc[i]
        return carry

    lax.fori_loop(0, shifted.shape[-1] // LANES, lane_block, 0)


def taps_coarse(shifted, field, out):
    def lane_block(lb, carry):
        lanes = pl.ds(pl.multiple_of(lb * LANES, LANES), LANES)
        v = [field[8 * i : 8 * i + 8, lanes] for i in range(8)]
        for b in range(7):
            acc = [None] * 7
            for ip in range(8):
                x = shifted[b, 8 * ip : 8 * ip + 8, lanes]
                for a in range(7):
                    i = ip - (a - 3)
                    if 0 <= i < 8:
                        acc[a] = x * v[i] if acc[a] is None else acc[a] + x * v[i]
            for a in range(7):
                t = 48 - (7 * a + b)
                out[t : t + 1, lanes] = jnp.sum(acc[a], axis=0, keepdims=True)
        return carry

    lax.fori_loop(0, shifted.shape[-1] // LANES, lane_block, 0)


def normalise(hidden):
    center = hidden - jnp.mean(hidden, axis=-1, keepdims=True)
    spread = jnp.mean(center * center, axis=-1, keepdims=True)
    scale = lax.rsqrt(spread + EPS)
    return center * scale, scale


def norm_back(grad, unit, scale, gain):
    g = grad * gain
    first = jnp.mean(g, axis=-1, keepdims=True)
    second = jnp.mean(g * unit, axis=-1, keepdims=True)
    return scale * (g - first - unit * second)


def gelu_pair(x):
    x2 = x * x
    t = jnp.tanh(x * (G0 + (G0 * G1) * x2))
    h = 0.5 + 0.5 * t
    act = x * h
    slope = h + act * (1.0 - t) * (G0 + (3.0 * G0 * G1) * x2)
    return act, slope


class Moves:
    def __init__(self, sems):
        self.sems = sems
        self.used = 0
        self.open = []

    def make(self, src, dst):
        copy = pltpu.make_async_copy(src, dst, self.sems.at[self.used])
        self.used += 1
        return copy

    def bring(self, src, dst):
        copy = self.make(src, dst)
        copy.start()
        return copy

    def pick(self, flag, src_if, src_else, dst):
        sem = self.sems.at[self.used]
        self.used += 1

        @pl.when(flag)
        def _():
            pltpu.make_async_copy(src_if, dst, sem).start()

        @pl.when(jnp.logical_not(flag))
        def _():
            pltpu.make_async_copy(src_else, dst, sem).start()

        return pltpu.make_async_copy(src_else, dst, sem)

    def send(self, src, dst):
        copy = self.make(src, dst)
        copy.start()
        self.open.append(copy)

    def finish(self):
        for copy in self.open:
            copy.wait()


def dot(a, b):
    return jnp.dot(a, b, preferred_element_type=F32)


def dot_nt(a, b):
    return lax.dot_general(a, b, NT, preferred_element_type=F32)


def forward_kernel(
    where,
    last1, last2, stem, recv,
    depth1, gains1, inner1, outer1, depth2, gains2, inner2, outer2, down, up,
    *rest,
):
    (
        send, t_two, t_one, t_r2, t_r1, t_d2, t_d1,
        patch, nrm2, act2, coarse, nrm1, act1,
        h1, h2, st, w_in1, w_out1, w_in2, w_out2, w_down, w_up,
        sh1, sh2, two, one, r2, r1, d2, d1,
        v_patch, v_nrm2, v_act2, v_coarse, v_nrm1, v_act1, p1, p2, sems,
    ) = rest[-39:]
    mv = Moves(sems)
    page, spot, first = where[0], where[1], where[2] == 1
    half = h2.shape[-1] // 2
    c_h1 = mv.pick(first, last1.at[page], recv.at[0:4], h1)
    c_h2 = [
        mv.pick(first, last2.at[page, :, half * s : half * s + half], recv.at[4 + s],
                h2.at[:, half * s : half * s + half])
        for s in range(2)
    ]
    c_down = mv.bring(down, w_down)
    c_in2 = mv.bring(inner2, w_in2)
    c_out2 = mv.bring(outer2, w_out2)
    c_up = mv.bring(up, w_up)
    c_st = mv.bring(stem.at[page], st)
    c_in1 = mv.bring(inner1, w_in1)
    c_out1 = mv.bring(outer1, w_out1)
    c1, c2 = h1.shape[-1], h2.shape[-1]

    c_h1.wait()
    c_down.wait()
    low = None
    for q in range(4):
        v_patch[q] = h1[q].astype(BF16)
        part = dot(v_patch[q], w_down[c1 * q : c1 * q + c1, :])
        low = part if low is None else low + part
    mv.send(v_patch, patch.at[spot])
    two[0] = low
    fill_coarse(sh2, low)
    conv_coarse(sh2, depth2, two.at[1], False)
    unit, scale = normalise(two[1])
    two[1] = unit
    r2[...] = jnp.broadcast_to(scale, r2.shape)
    v_nrm2[...] = (unit * gains2[0:1, :]).astype(BF16)
    mv.send(v_nrm2, nrm2.at[spot])
    mv.send(r2, t_r2)
    c_in2.wait()
    wide2 = w_in2.shape[-1]
    for n in range(0, wide2, 512):
        a, s = gelu_pair(dot(v_nrm2[...], w_in2[:, n : n + 512]))
        v_act2[:, n : n + 512] = a.astype(BF16)
        d2[:, n : n + 512] = s.astype(BF16)
    mv.send(v_act2, act2.at[spot])
    mv.send(d2, t_d2)
    c_out2.wait()
    out2 = dot(v_act2[...], w_out2[...])
    two[2] = out2
    for copy in c_h2:
        copy.wait()
    prev2 = (h2[...] - gains2[1:2, :] * out2) / gains2[2:3, :]
    p2[...] = prev2
    mv.send(two, t_two)
    for s in range(2):
        mv.send(p2.at[:, half * s : half * s + half], send.at[4 + s])
    v_coarse[...] = prev2.astype(BF16)
    mv.send(v_coarse, coarse.at[spot])
    c_up.wait()
    lift = dot(v_coarse[...], w_up[...])
    c_st.wait()
    for q in range(4):
        entry = st[q].astype(F32) + lift
        one[0, q] = entry
        fill_fine(sh1, entry, q)
    conv_fine(sh1, depth1, one.at[1], False)
    for q in range(4):
        unit, scale = normalise(one[1, q])
        one[1, q] = unit
        r1[q] = jnp.broadcast_to(scale, r1.shape[1:])
        v_nrm1[64 * q : 64 * q + 64, :] = (unit * gains1[0:1, :]).astype(BF16)
    mv.send(v_nrm1, nrm1.at[spot])
    mv.send(r1, t_r1)
    c_in1.wait()
    wide1 = w_in1.shape[-1]
    for n in range(0, wide1, 256):
        a, s = gelu_pair(dot(v_nrm1[...], w_in1[:, n : n + 256]))
        v_act1[:, n : n + 256] = a.astype(BF16)
        d1[:, n : n + 256] = s.astype(BF16)
    mv.send(v_act1, act1.at[spot])
    mv.send(d1, t_d1)
    c_out1.wait()
    for q in range(4):
        out1 = dot(v_act1[64 * q : 64 * q + 64, :], w_out1[...])
        one[2, q] = out1
        p1[q] = (h1[q] - gains1[1:2, :] * out1) / gains1[2:3, :]
    mv.send(one, t_one)
    mv.send(p1, send.at[0:4])
    mv.finish()


def backward_kernel(
    where,
    last1, last2, teach1, teach2, recv, prev, t_two, t_one, t_r2, t_r1, t_d2, t_d1,
    depth1, gains1, inner1, outer1, depth2, gains2, inner2, outer2, down, up,
    *rest,
):
    (
        send, gout2, gpre2, glow, gout1, gpre1, gpool, stem, small,
        g1, g2, te1, te2, p1, p2, two, one, r2, r1, d2, d1,
        w_in1, w_out1, w_in2, w_out2, w_down, w_up,
        sh1, sh2, low_g, ent_g,
        v_gout2, v_gpre2, v_glow, v_gout1, v_gpre1, v_gpool, v_small, n1, n2,
        sems,
    ) = rest[-41:]
    mv = Moves(sems)
    v_small[...] = jnp.zeros_like(v_small)
    page, spot, first, slot = where[0], where[1], where[2] == 1, where[3]
    half = g2.shape[-1] // 2
    c1, c2 = g1.shape[-1], g2.shape[-1]
    c_g2 = [
        mv.pick(first, last2.at[page, :, half * s : half * s + half], recv.at[4 + s],
                g2.at[:, half * s : half * s + half])
        for s in range(2)
    ]
    c_te2 = mv.bring(teach2.at[slot], te2)
    c_out2 = mv.bring(outer2, w_out2)
    c_d2 = mv.bring(t_d2, d2)
    c_two = mv.bring(t_two, two)
    c_in2 = mv.bring(inner2, w_in2)
    c_r2 = mv.bring(t_r2, r2)
    c_p2 = [mv.bring(prev.at[4 + s], p2.at[:, half * s : half * s + half]) for s in range(2)]
    c_g1 = mv.pick(first, last1.at[page], recv.at[0:4], g1)
    c_te1 = mv.bring(teach1.at[slot], te1)
    c_down = mv.bring(down, w_down)
    c_p1 = mv.bring(prev.at[0:4], p1)
    c_one = mv.bring(t_one, one)
    c_out1 = mv.bring(outer1, w_out1)
    c_d1 = mv.bring(t_d1, d1)
    c_in1 = mv.bring(inner1, w_in1)
    c_r1 = mv.bring(t_r1, r1)
    c_up = mv.bring(up, w_up)

    for copy in c_g2:
        copy.wait()
    c_te2.wait()

    @pl.when(first)
    def _():
        g2[...] = (g2[...] - te2[...].astype(F32)) / 8.0

    v_gout2[...] = (gains2[1:2, :] * g2[...]).astype(BF16)
    mv.send(v_gout2, gout2.at[spot])
    c_out2.wait()
    c_d2.wait()
    wide2 = w_in2.shape[-1]
    for n in range(0, wide2, 512):
        part = dot_nt(v_gout2[...], w_out2[n : n + 512, :])
        v_gpre2[:, n : n + 512] = (part * d2[:, n : n + 512].astype(F32)).astype(BF16)
    mv.send(v_gpre2, gpre2.at[spot])
    c_in2.wait()
    gn = dot_nt(v_gpre2[...], w_in2[...])
    c_two.wait()
    c_r2.wait()
    for copy in c_p2:
        copy.wait()
    unit = two[1]
    v_small[56:57, :] = jnp.sum(gn * unit, axis=0, keepdims=True)
    v_small[57:58, :] = jnp.sum(g2[...] * two[2], axis=0, keepdims=True)
    v_small[58:59, :] = jnp.sum(g2[...] * p2[...], axis=0, keepdims=True)
    fill_coarse(sh2, norm_back(gn, unit, r2[:, 0:1], gains2[0:1, :]))
    conv_coarse(sh2, depth2, low_g, True)
    v_glow[...] = low_g[...].astype(BF16)
    mv.send(v_glow, glow.at[spot])
    taps_coarse(sh2, two.at[0], v_small.at[0:56])
    c_g1.wait()
    c_te1.wait()

    @pl.when(first)
    def _():
        for q in range(4):
            g1[q] = (g1[q] - te1[q].astype(F32)) / 16.0

    c_down.wait()
    c_p1.wait()
    c_one.wait()
    gamma = jnp.zeros((1, c1), F32)
    layer = jnp.zeros((1, c1), F32)
    for q in range(4):
        total = g1[q] + dot_nt(v_glow[...], w_down[c1 * q : c1 * q + c1, :])
        gamma += jnp.sum(total * p1[q], axis=0, keepdims=True)
        layer += jnp.sum(total * one[2, q], axis=0, keepdims=True)
        v_gout1[64 * q : 64 * q + 64, :] = (gains1[1:2, :] * total).astype(BF16)
        n1[q] = gains1[2:3, :] * total
    mv.send(n1, send.at[0:4])
    mv.send(v_gout1, gout1.at[spot])
    c_out1.wait()
    c_d1.wait()
    wide1 = w_in1.shape[-1]
    for n in range(0, wide1, 256):
        part = dot_nt(v_gout1[...], w_out1[n : n + 256, :])
        v_gpre1[:, n : n + 256] = (part * d1[:, n : n + 256].astype(F32)).astype(BF16)
    mv.send(v_gpre1, gpre1.at[spot])
    c_in1.wait()
    c_r1.wait()
    ggain = jnp.zeros((1, c1), F32)
    for q in range(4):
        gn = dot_nt(v_gpre1[64 * q : 64 * q + 64, :], w_in1[...])
        unit = one[1, q]
        ggain += jnp.sum(gn * unit, axis=0, keepdims=True)
        fill_fine(sh1, norm_back(gn, unit, r1[q, :, 0:1], gains1[0:1, :]), q)
    v_small[120:121, 0:c1] = ggain
    v_small[121:122, 0:c1] = layer
    v_small[122:123, 0:c1] = gamma
    conv_fine(sh1, depth1, ent_g, True)
    mv.send(ent_g, stem.at[spot])
    v_gpool[...] = (ent_g[0] + ent_g[1] + ent_g[2] + ent_g[3]).astype(BF16)
    mv.send(v_gpool, gpool.at[spot])
    c_up.wait()
    n2[...] = gains2[2:3, :] * g2[...] + dot_nt(v_gpool[...], w_up[...])
    for s in range(2):
        mv.send(n2.at[:, half * s : half * s + half], send.at[4 + s])
    taps_fine(sh1, one.at[0], v_small.at[64:120, 0:c1])
    mv.send(v_small, small.at[spot])
    mv.finish()


ANY = pl.BlockSpec(memory_space=pl.ANY)
SMEM = pl.BlockSpec(memory_space=pltpu.SMEM)
INSIDE = pl.BlockSpec(memory_space=pltpu.VMEM)
VMEM_LIMIT = 48 * 1024 * 1024


def sds(shape, dtype):
    return jax.ShapeDtypeStruct(tuple(shape), dtype)


def page_sizes(weights):
    depth1, gains1, inner1, outer1, depth2, gains2, inner2, outer2, down, up = weights
    return gains1.shape[-1], gains2.shape[-1], inner1.shape[-1], inner2.shape[-1]


def forward_call(where, fields, recv, weights, kept, stacks):
    c1, c2, e1, e2 = page_sizes(weights)
    last1, last2, stem = fields
    temps = [
        sds(recv.shape, F32), sds((3, 64, c2), F32), sds((3, 4, 64, c1), F32),
        sds((64, LANES), F32), sds((4, 64, LANES), F32), sds((64, e2), BF16), sds((256, e1), BF16),
    ]
    out_shape = temps + list(kept)
    wspecs = [INSIDE, INSIDE, ANY, ANY, INSIDE, INSIDE, ANY, ANY, ANY, ANY]
    in_specs = [SMEM] + [ANY] * 4 + wspecs + [ANY] * len(stacks)
    first_stack = 5 + len(weights)
    scratch = [
        pltpu.VMEM((4, 64, c1), F32), pltpu.VMEM((64, c2), F32), pltpu.VMEM((4, 64, c1), BF16),
        pltpu.VMEM((c1, e1), BF16), pltpu.VMEM((e1, c1), BF16),
        pltpu.VMEM((c2, e2), BF16), pltpu.VMEM((e2, c2), BF16),
        pltpu.VMEM((4 * c1, c2), BF16), pltpu.VMEM((c2, c1), BF16),
        pltpu.VMEM((4, 4, 64, c1), F32), pltpu.VMEM((7, 64, c2), F32),
        pltpu.VMEM((3, 64, c2), F32), pltpu.VMEM((3, 4, 64, c1), F32),
        pltpu.VMEM((64, LANES), F32), pltpu.VMEM((4, 64, LANES), F32),
        pltpu.VMEM((64, e2), BF16), pltpu.VMEM((256, e1), BF16),
    ]
    scratch += [pltpu.VMEM(s.shape[1:], s.dtype) for s in kept]
    scratch += [pltpu.VMEM((4, 64, c1), F32), pltpu.VMEM((64, c2), F32)]
    scratch += [pltpu.SemaphoreType.DMA((40,))]
    macs = 64 * (4 * c1 * c2 + 2 * c2 * e2 + c2 * c1) + 256 * 2 * c1 * e1
    outs = pl.pallas_call(
        forward_kernel,
        out_shape=out_shape,
        in_specs=in_specs,
        out_specs=[ANY] * len(out_shape),
        scratch_shapes=scratch,
        input_output_aliases={first_stack + k: len(temps) + k for k in range(len(stacks))},
        compiler_params=pltpu.CompilerParams(vmem_limit_bytes=VMEM_LIMIT),
        cost_estimate=pl.CostEstimate(flops=2 * macs, bytes_accessed=20 << 20, transcendentals=0),
        name="forward_page",
    )(where, last1, last2, stem, recv, *weights, *stacks)
    return outs[0], outs[1 : len(temps)], tuple(outs[len(temps) :])


def backward_call(where, fields, recv, prev, temps, weights, kept, stacks):
    c1, c2, e1, e2 = page_sizes(weights)
    last1, last2, teach1, teach2 = fields
    out_shape = [sds(recv.shape, F32)] + list(kept)
    wspecs = [INSIDE, INSIDE, ANY, ANY, INSIDE, INSIDE, ANY, ANY, ANY, ANY]
    lead = 1 + 4 + 2 + len(temps)
    in_specs = [SMEM] + [ANY] * (lead - 1) + wspecs + [ANY] * len(stacks)
    first_stack = lead + len(weights)
    scratch = [
        pltpu.VMEM((4, 64, c1), F32), pltpu.VMEM((64, c2), F32),
        pltpu.VMEM((4, 64, c1), BF16), pltpu.VMEM((64, c2), BF16),
        pltpu.VMEM((4, 64, c1), F32), pltpu.VMEM((64, c2), F32),
    ]
    scratch += [pltpu.VMEM(t.shape, t.dtype) for t in temps]
    scratch += [
        pltpu.VMEM((c1, e1), BF16), pltpu.VMEM((e1, c1), BF16),
        pltpu.VMEM((c2, e2), BF16), pltpu.VMEM((e2, c2), BF16),
        pltpu.VMEM((4 * c1, c2), BF16), pltpu.VMEM((c2, c1), BF16),
        pltpu.VMEM((4, 4, 64, c1), F32), pltpu.VMEM((7, 64, c2), F32),
        pltpu.VMEM((64, c2), F32), pltpu.VMEM((4, 64, c1), F32),
    ]
    held = [pltpu.VMEM(s.shape[1:], s.dtype) for s in kept]
    scratch += held[:6] + held[7:]
    scratch += [pltpu.VMEM((4, 64, c1), F32), pltpu.VMEM((64, c2), F32)]
    scratch += [pltpu.SemaphoreType.DMA((48,))]
    macs = 64 * (4 * c1 * c2 + 2 * c2 * e2 + c2 * c1) + 256 * 2 * c1 * e1
    outs = pl.pallas_call(
        backward_kernel,
        out_shape=out_shape,
        in_specs=in_specs,
        out_specs=[ANY] * len(out_shape),
        scratch_shapes=scratch,
        input_output_aliases={first_stack + k: 1 + k for k in range(len(stacks))},
        compiler_params=pltpu.CompilerParams(vmem_limit_bytes=VMEM_LIMIT),
        cost_estimate=pl.CostEstimate(flops=2 * macs, bytes_accessed=20 << 20, transcendentals=0),
        name="backward_page",
    )(where, last1, last2, teach1, teach2, recv, prev, *temps, *weights, *stacks)
    return outs[0], tuple(outs[1:])


def to_phases(field):
    pages, side, _, channels = field.shape
    half = side // 2
    shaped = field.reshape(pages, half, 2, half, 2, channels)
    return shaped.transpose(0, 2, 4, 1, 3, 5).reshape(pages, 4, half * half, channels)


def from_phases(field, side):
    pages, _, cells, channels = field.shape
    half = side // 2
    shaped = field.reshape(pages, 2, 2, half, half, channels)
    return shaped.transpose(0, 3, 1, 4, 2, 5).reshape(pages, side, side, channels)


def kept_shapes(pages, c1, c2, e1, e2):
    n = pages + 1
    ahead = (
        sds((n, 4, 64, c1), BF16), sds((n, 64, c2), BF16), sds((n, 64, e2), BF16),
        sds((n, 64, c2), BF16), sds((n, 256, c1), BF16), sds((n, 256, e1), BF16),
    )
    back = (
        sds((n, 64, c2), BF16), sds((n, 64, e2), BF16), sds((n, 64, c2), BF16),
        sds((n, 256, c1), BF16), sds((n, 256, e1), BF16), sds((n, 64, c1), BF16),
        sds((n, 4, 64, c1), F32), sds((n, 128, c2), F32),
    )
    return ahead, back


def plan(c1, c2, e1, e2, pieces):
    whole = (e2 // 2, c2 * e2 // (2 * c2), 2 * c1, c1 * e1 // (2 * c2), c1 * e1 // (2 * c2), c1 // 2)
    rows = [n // pieces for n in whole] + [8]
    starts = [sum(rows[:k]) for k in range(len(rows) + 1)]
    return rows, starts


def piece_index(bits, masks_count, group, rel):
    index = jnp.int32(group)
    for s in range(masks_count):
        own = bits[s if group == 0 else masks_count - 1 - s]
        index = 2 * index + (own + rel[s]) % 2
    return index


def rel_bits(value, count):
    return tuple((value >> (count - 1 - s)) & 1 for s in range(count))


def weight_kernel(levels, pages, sizes, where, *refs):
    c1, c2, e1, e2 = sizes
    pieces = 2 << levels
    rows, starts = plan(c1, c2, e1, e2, pieces)
    (
        patch, nrm2, act2, coarse, nrm1, act1, gout2, gpre2, glow, gout1, gpre1, gpool, small,
        first, later,
        v_patch, v_nrm2, v_act2, v_coarse, v_nrm1, v_act1,
        v_gout2, v_gpre2, v_glow, v_gout1, v_gpre1, v_gpool, v_small, flat, sems,
    ) = refs
    mv = Moves(sems)
    half = where[0]
    bits = [where[1 + s] for s in range(levels)]

    def part(ref, width):
        return ref.at[0:pages, :, pl.ds(pl.multiple_of(half * width, width), width)]

    w_act1 = mv.bring(part(act1, e1 // 2), v_act1)
    w_gout1 = mv.bring(gout1.at[0:pages], v_gout1)
    w_nrm1 = mv.bring(nrm1.at[0:pages], v_nrm1)
    w_gpre1 = mv.bring(part(gpre1, e1 // 2), v_gpre1)
    w_act2 = mv.bring(part(act2, e2 // 2), v_act2)
    w_gout2 = mv.bring(gout2.at[0:pages], v_gout2)
    w_nrm2 = mv.bring(nrm2.at[0:pages], v_nrm2)
    w_gpre2 = mv.bring(part(gpre2, e2 // 2), v_gpre2)
    w_patch = mv.bring(patch.at[0:pages, pl.ds(2 * half, 2)], v_patch)
    w_glow = mv.bring(glow.at[0:pages], v_glow)
    w_coarse = mv.bring(part(coarse, c2 // 2), v_coarse)
    w_gpool = mv.bring(gpool.at[0:pages], v_gpool)
    w_small = mv.bring(small.at[0:pages, pl.ds(pl.multiple_of(64 * half, 64), 64)], v_small)

    def flatten(value):
        return value.reshape(-1, value.shape[-1])

    def product(left, right):
        return lax.dot_general(left, right, (((0,), (0,)), ((), ())), preferred_element_type=F32)

    def place(section, row, value, lane=0):
        size = rows[section]
        done = 0
        while done < value.shape[0]:
            p, inside = divmod(row + done, size)
            count = min(size - inside, value.shape[0] - done)
            at = starts[section] + inside
            flat[p, at : at + count, lane : lane + value.shape[1]] = value[done : done + count]
            done += count

    w_act1.wait()
    w_gout1.wait()
    right = flatten(v_gout1[...])
    lanes = c2 // c1
    run = e1 // 2 // lanes
    for k in range(lanes):
        place(4, 0, product(flatten(v_act1[:, :, run * k : run * k + run]), right), c1 * k)
    w_nrm1.wait()
    w_gpre1.wait()
    left = flatten(v_nrm1[...])
    for k in range(e1 // 2 // c2):
        place(3, c1 * k, product(left, flatten(v_gpre1[:, :, c2 * k : c2 * k + c2])))
    w_act2.wait()
    w_gout2.wait()
    right = flatten(v_gout2[...])
    for r in range(0, e2 // 2, 256):
        place(0, r, product(flatten(v_act2[:, :, r : r + 256]), right))
    w_nrm2.wait()
    w_gpre2.wait()
    for k in range(e2 // 2 // c2):
        right = flatten(v_gpre2[:, :, c2 * k : c2 * k + c2])
        for r in range(0, c2, 256):
            place(1, c2 * k + r, product(flatten(v_nrm2[:, :, r : r + 256]), right))
    w_patch.wait()
    w_glow.wait()
    right = flatten(v_glow[...])
    for q in range(2):
        place(2, c1 * q, product(flatten(v_patch[:, q]), right))
    w_coarse.wait()
    w_gpool.wait()
    right = flatten(v_gpool[...])
    run = c2 // 2 // lanes
    for k in range(lanes):
        place(5, 0, product(flatten(v_coarse[:, :, run * k : run * k + run]), right), c1 * k)
    w_small.wait()
    total = v_small[0]
    for p in range(1, pages):
        total = total + v_small[p]
    for p in range(min(pieces, total.shape[0] // 8)):
        flat[p, starts[6] : starts[7], :] = total[8 * p : 8 * p + 8]
    for p in range(total.shape[0] // 8, pieces):
        flat[p, starts[6] : starts[7], :] = jnp.zeros((8, c2), F32)
    slot = 0
    each = pieces // 4
    for group in range(2):
        for value in range(2 * each):
            rel = rel_bits(value, levels)
            index = piece_index(bits, levels, group, rel)
            out = first if rel[0] == 1 else later
            mv.send(flat.at[index], out.at[each * group + value % each])
    mv.finish()


def weight_call(where, levels, pages, sizes, arrays):
    c1, c2, e1, e2 = sizes
    pieces = 2 << levels
    rows, starts = plan(c1, c2, e1, e2, pieces)
    scratch = [
        pltpu.VMEM((pages, 2, 64, c1), BF16), pltpu.VMEM((pages, 64, c2), BF16),
        pltpu.VMEM((pages, 64, e2 // 2), BF16), pltpu.VMEM((pages, 64, c2 // 2), BF16),
        pltpu.VMEM((pages, 256, c1), BF16), pltpu.VMEM((pages, 256, e1 // 2), BF16),
        pltpu.VMEM((pages, 64, c2), BF16), pltpu.VMEM((pages, 64, e2 // 2), BF16),
        pltpu.VMEM((pages, 64, c2), BF16), pltpu.VMEM((pages, 256, c1), BF16),
        pltpu.VMEM((pages, 256, e1 // 2), BF16), pltpu.VMEM((pages, 64, c1), BF16),
        pltpu.VMEM((pages, 64, c2), F32), pltpu.VMEM((pieces, starts[7], c2), F32),
        pltpu.SemaphoreType.DMA((16 + pieces,)),
    ]
    out = sds((pieces // 2, starts[7], c2), F32)
    macs = pages * (64 * (c1 * 4 * c2 + 2 * c2 * e2 + c2 * c1) + 256 * 2 * c1 * e1) // 2

    def kernel(*refs):
        weight_kernel(levels, pages, sizes, *refs)

    return pl.pallas_call(
        kernel,
        out_shape=[out, out],
        in_specs=[SMEM] + [ANY] * len(arrays),
        out_specs=[ANY, ANY],
        scratch_shapes=scratch,
        compiler_params=pltpu.CompilerParams(vmem_limit_bytes=VMEM_LIMIT),
        cost_estimate=pl.CostEstimate(flops=2 * macs, bytes_accessed=14 << 20, transcendentals=0),
        name="weight_half",
    )(where, *arrays)


def spread_kernel(levels, sizes, keys, where, *refs):
    c1, c2, e1, e2 = sizes
    pieces = 2 << levels
    rows, starts = plan(c1, c2, e1, e2, pieces)
    n = len(keys)
    parts = refs[:n]
    in1, out1, in2, out2, down, up, k1, s1, k2, s2, sems, done = refs[-12:]
    tail = done
    bits = [where[1 + s] for s in range(levels)]
    lanes = c2 // c1
    waits = []
    for k, (core, group, rel) in enumerate(keys):
        half = (where[0] + core) % 2
        p = piece_index(bits, levels, group, rel)
        src, sem = parts[k], sems.at[k]

        def go(section, dst, lane=None, src=src, sem=sem):
            piece = src.at[starts[section] : starts[section + 1]]
            if lane is not None:
                piece = piece.at[:, c1 * lane : c1 * lane + c1]
            pltpu.make_async_copy(piece, dst, sem).start()

        def span(base, count):
            return pl.ds(pl.multiple_of(base, count), count)

        go(0, out2.at[span(half * (e2 // 2) + rows[0] * p, rows[0]), :])
        per = c2 // rows[1]
        go(1, in2.at[
            span((p % per) * rows[1], rows[1]),
            span(half * (e2 // 2) + c2 * (p // per), c2),
        ])
        go(2, down.at[span(half * (2 * c1) + rows[2] * p, rows[2]), :])
        go(3, in1.at[span(rows[3] * p, rows[3]), span(half * (e1 // 2), c2)])
        for k2_ in range(lanes):
            run = e1 // 2 // lanes
            go(4, out1.at[span(half * (e1 // 2) + run * k2_ + rows[4] * p, rows[4]), :], k2_)
            run = c2 // 2 // lanes
            go(5, up.at[span(half * (c2 // 2) + run * k2_ + rows[5] * p, rows[5]), :], k2_)
        go(6, tail.at[span(pieces * 8 * half + 8 * p, 8), :])
        waits.append(pltpu.make_async_copy(src, src, sem))
    for copy in waits:
        copy.wait()
    base = [0, pieces * 8]
    k2[...] = tail[0:49, :]
    s2[...] = tail[56:64, :]
    k1[...] = tail[base[1] : base[1] + 49, 0:c1]
    s1[...] = tail[base[1] + 56 : base[1] + 64, 0:c1]


def spread_call(where, levels, sizes, table):
    c1, c2, e1, e2 = sizes
    pieces = 2 << levels
    keys = sorted(table)
    parts = [table[k] for k in keys]
    outs = [
        sds((c1, e1), F32), sds((e1, c1), F32), sds((c2, e2), F32), sds((e2, c2), F32),
        sds((4 * c1, c2), F32), sds((c2, c1), F32),
        sds((49, c1), F32), sds((8, c1), F32), sds((49, c2), F32), sds((8, c2), F32),
    ]

    def kernel(*refs):
        spread_kernel(levels, sizes, keys, *refs)

    return pl.pallas_call(
        kernel,
        out_shape=outs,
        in_specs=[SMEM] + [ANY] * len(parts),
        out_specs=[ANY] * 6 + [INSIDE] * 4,
        scratch_shapes=[pltpu.SemaphoreType.DMA((len(parts),)), pltpu.VMEM((16 * pieces, c2), F32)],
        compiler_params=pltpu.CompilerParams(vmem_limit_bytes=VMEM_LIMIT),
        cost_estimate=pl.CostEstimate(flops=0, bytes_accessed=26 << 20, transcendentals=0),
        name="spread",
    )(where, *parts)


def swap(value, mask):
    return lax.ppermute(value, "dp", [(i, i ^ mask) for i in range(lax.axis_size("dp"))])


def sum_weights(arrays, pages, sizes):
    devices = lax.axis_size("dp")
    levels = devices.bit_length() - 2
    index = lax.axis_index("dp")
    masks = [2 << s for s in range(levels)]
    order = [masks, masks[::-1]]
    core = index % 2
    bits = [(index // m) % 2 for m in masks]
    where = jnp.stack([core] + bits).astype(jnp.int32)
    other = jnp.stack([1 - core] + bits).astype(jnp.int32)
    their_first, their_later = weight_call(other, levels, pages, sizes, arrays)
    got_first = swap(their_first, 1)
    my_first, my_later = weight_call(where, levels, pages, sizes, arrays)
    got_later = swap(their_later, 1)
    each = 1 << (levels - 1)
    held = {}
    for group in range(2):
        for value in range(2 * each):
            rel = rel_bits(value, levels)
            mine, got = (my_first, got_first) if rel[0] else (my_later, got_later)
            k = each * group + value % each
            held[group, rel] = mine[k] + got[k]
    for s in range(levels):
        for value in reversed(range(1 << (levels - 1 - s))):
            for group in range(2):
                rest = rel_bits(value, levels - 1 - s)
                there, here = (0,) * s + (1,) + rest, (0,) * (s + 1) + rest
                arrived = swap(held.pop((group, there)), order[group][s])
                held[group, here] = held[group, here] + arrived
    table = {}

    def keep(group, rel, value):
        table[0, group, rel] = value
        table[1, group, rel] = swap(value, 1)

    for group in range(2):
        keep(group, (0,) * levels, held[group, (0,) * levels])
    for s in reversed(range(levels)):
        for value in range(1 << (levels - 1 - s)):
            for group in range(2):
                rest = rel_bits(value, levels - 1 - s)
                here, there = (0,) * (s + 1) + rest, (0,) * s + (1,) + rest
                keep(group, there, swap(table[0, group, here], order[group][s]))
    return spread_call(where, levels, sizes, table)


def local(
    stem_map, last_one, last_two, teach_one, teach_two, teacher_slot,
    depth_one, gains_one, inner_one, outer_one, depth_two, gains_two, inner_two, outer_two,
    down_proj, up_proj,
):
    columns = lax.axis_size("col")
    position = lax.axis_index("col")
    pages, side = stem_map.shape[0], stem_map.shape[1]
    c1, c2 = last_one.shape[-1], last_two.shape[-1]
    sizes = (c1, c2, inner_one.shape[-1], inner_two.shape[-1])
    last1 = to_phases(last_one)
    last2 = last_two.reshape(pages, 64, c2)
    stem = to_phases(stem_map)
    teach1 = to_phases(teach_one)
    teach2 = teach_two.reshape(pages, 64, c2)
    weights = (
        depth_one[0].astype(F32), gains_one[0], inner_one[0], outer_one[0],
        depth_two[0].astype(F32), gains_two[0], inner_two[0], outer_two[0],
        down_proj[0], up_proj[0],
    )
    first = (position == columns - 1).astype(jnp.int32)
    route = [(i, i - 1) for i in range(1, columns)]
    ahead_shapes, back_shapes = kept_shapes(pages, *sizes)
    blank = jnp.zeros((6, 64, c1), F32)

    def slot(k, out_grad, recv_high, ahead, back):
        micro = k - (columns - 1 - position)
        active = jnp.logical_and(micro >= 0, micro < pages)
        page = jnp.clip(micro, 0, pages - 1)
        spot = jnp.where(active, micro, pages)
        where = jnp.stack([page, spot, first, teacher_slot[page]]).astype(jnp.int32)
        recv_grad = blank if out_grad is None else lax.ppermute(out_grad, "col", route)
        prev, temps, ahead = forward_call(
            where, (last1, last2, stem), recv_high, weights, ahead_shapes, ahead
        )
        next_high = lax.ppermute(prev, "col", route)
        out_grad, back = backward_call(
            where, (last1, last2, teach1, teach2), recv_grad, prev, temps, weights,
            back_shapes, back,
        )
        return out_grad, next_high, ahead, back

    begun = slot(jnp.int32(0), None, blank, (), ())
    _, _, ahead, back = lax.fori_loop(
        1, columns + pages - 1, lambda k, carried: slot(k, *carried), begun
    )
    stem_total = from_phases(lax.psum(back[6][:pages], "col"), side)
    in1, out1, in2, out2, down, up, k1, s1, k2, s2 = sum_weights(
        ahead + back[:6] + back[7:], pages, sizes
    )
    return (
        k1[None], s1[None, :3], in1[None], out1[None], k2[None], s2[None, :2], s2[2:3],
        in2[None], out2[None], down[None], up[None], stem_total,
    )


def solution(mesh):
    paged, row, mat = P("dp", None, None, None), P("col", None), P("col", None, None)
    return jax.shard_map(
        local,
        mesh=mesh,
        in_specs=(paged,) * 5 + (P("dp"),) + (mat,) * 10,
        out_specs=(mat,) * 6 + (row,) + (mat,) * 4 + (paged,),
        check_vma=False,
    )
```

```python
import functools

import jax
import jax.numpy as jnp
from jax import lax
from jax.experimental import pallas as pl
from jax.experimental.pallas import tpu as pltpu
from jax.sharding import PartitionSpec as P

F32 = jnp.float32
BF16 = jnp.bfloat16
LANES = 128
EPS = 1e-06
G0 = 0.7978845608028654
G1 = 0.044715
NT = (((1,), (1,)), ((), ()))


def shift_rows(block, step):
    if step == 0:
        return block
    rolled = pltpu.roll(block, (-step) % 8, 0)
    place = lax.broadcasted_iota(jnp.int32, block.shape, 0) + step
    return jnp.where((place >= 0) & (place < 8), rolled, 0.0)


def fine_shifts(col_parity):
    return (-1, 0, 1, 2) if col_parity == 0 else (-2, -1, 0, 1)


def fill_fine(shifted, value, phase):
    for row in range(8):
        line = value[8 * row : 8 * row + 8]
        for k, step in enumerate(fine_shifts(phase & 1)):
            shifted[k, phase, 8 * row : 8 * row + 8, :] = shift_rows(line, step)


def fill_coarse(shifted, value):
    for row in range(8):
        line = value[8 * row : 8 * row + 8]
        for k in range(7):
            shifted[k, 8 * row : 8 * row + 8, :] = shift_rows(line, k - 3)


def fine_source(dj, b):
    off = dj + b - 3
    pj = off & 1
    step = (off - pj) // 2
    return pj, step + (1 if pj == 0 else 2)


def conv_fine(shifted, taps, out, flip):
    def lane_block(lb, carry):
        lanes = pl.ds(pl.multiple_of(lb * LANES, LANES), LANES)
        for dj in range(2):
            acc = [None] * 16
            for b in range(7):
                pj, k = fine_source(dj, b)
                w = []
                for a in range(7):
                    t = 48 - (7 * a + b) if flip else 7 * a + b
                    w.append(jnp.broadcast_to(taps[t : t + 1, lanes], (8, LANES)))
                for ip in range(16):
                    r = 8 * (ip >> 1)
                    x = shifted[k, 2 * (ip & 1) + pj, r : r + 8, lanes]
                    for a in range(7):
                        i = ip - (a - 3)
                        if 0 <= i < 16:
                            acc[i] = x * w[a] if acc[i] is None else acc[i] + x * w[a]
            for i in range(16):
                r = 8 * (i >> 1)
                out[2 * (i & 1) + dj, r : r + 8, lanes] = acc[i]
        return carry

    lax.fori_loop(0, shifted.shape[-1] // LANES, lane_block, 0)


def taps_fine(shifted, field, out):
    def lane_block(lb, carry):
        lanes = pl.ds(pl.multiple_of(lb * LANES, LANES), LANES)
        for b in range(7):
            acc = [None] * 7
            for dj in range(2):
                pj, k = fine_source(dj, b)
                v = [
                    field[2 * (i & 1) + dj, 8 * (i >> 1) : 8 * (i >> 1) + 8, lanes]
                    for i in range(16)
                ]
                for ip in range(16):
                    r = 8 * (ip >> 1)
                    x = shifted[k, 2 * (ip & 1) + pj, r : r + 8, lanes]
                    for a in range(7):
                        i = ip - (a - 3)
                        if 0 <= i < 16:
                            acc[a] = x * v[i] if acc[a] is None else acc[a] + x * v[i]
            for a in range(7):
                t = 48 - (7 * a + b)
                out[t : t + 1, lanes] = jnp.sum(acc[a], axis=0, keepdims=True)
        return carry

    lax.fori_loop(0, shifted.shape[-1] // LANES, lane_block, 0)


def conv_coarse(shifted, taps, out, flip):
    def lane_block(lb, carry):
        lanes = pl.ds(pl.multiple_of(lb * LANES, LANES), LANES)
        acc = [None] * 8
        for b in range(7):
            w = []
            for a in range(7):
                t = 48 - (7 * a + b) if flip else 7 * a + b
                w.append(jnp.broadcast_to(taps[t : t + 1, lanes], (8, LANES)))
            for ip in range(8):
                x = shifted[b, 8 * ip : 8 * ip + 8, lanes]
                for a in range(7):
                    i = ip - (a - 3)
                    if 0 <= i < 8:
                        acc[i] = x * w[a] if acc[i] is None else acc[i] + x * w[a]
        for i in range(8):
            out[8 * i : 8 * i + 8, lanes] = acc[i]
        return carry

    lax.fori_loop(0, shifted.shape[-1] // LANES, lane_block, 0)


def taps_coarse(shifted, field, out):
    def lane_block(lb, carry):
        lanes = pl.ds(pl.multiple_of(lb * LANES, LANES), LANES)
        v = [field[8 * i : 8 * i + 8, lanes] for i in range(8)]
        for b in range(7):
            acc = [None] * 7
            for ip in range(8):
                x = shifted[b, 8 * ip : 8 * ip + 8, lanes]
                for a in range(7):
                    i = ip - (a - 3)
                    if 0 <= i < 8:
                        acc[a] = x * v[i] if acc[a] is None else acc[a] + x * v[i]
            for a in range(7):
                t = 48 - (7 * a + b)
                out[t : t + 1, lanes] = jnp.sum(acc[a], axis=0, keepdims=True)
        return carry

    lax.fori_loop(0, shifted.shape[-1] // LANES, lane_block, 0)


def normalise(hidden):
    center = hidden - jnp.mean(hidden, axis=-1, keepdims=True)
    spread = jnp.mean(center * center, axis=-1, keepdims=True)
    scale = lax.rsqrt(spread + EPS)
    return center * scale, scale


def norm_back(grad, unit, scale, gain):
    g = grad * gain
    first = jnp.mean(g, axis=-1, keepdims=True)
    second = jnp.mean(g * unit, axis=-1, keepdims=True)
    return scale * (g - first - unit * second)


def gelu_pair(x):
    x2 = x * x
    t = jnp.tanh(x * (G0 + (G0 * G1) * x2))
    h = 0.5 + 0.5 * t
    act = x * h
    slope = h + act * (1.0 - t) * (G0 + (3.0 * G0 * G1) * x2)
    return act, slope


class Moves:
    def __init__(self, sems):
        self.sems = sems
        self.used = 0
        self.open = []

    def make(self, src, dst):
        copy = pltpu.make_async_copy(src, dst, self.sems.at[self.used])
        self.used += 1
        return copy

    def bring(self, src, dst):
        copy = self.make(src, dst)
        copy.start()
        return copy

    def send(self, src, dst):
        copy = self.make(src, dst)
        copy.start()
        self.open.append(copy)

    def finish(self):
        for copy in self.open:
            copy.wait()


def dot(a, b):
    return jnp.dot(a, b, preferred_element_type=F32)


def dot_nt(a, b):
    return lax.dot_general(a, b, NT, preferred_element_type=F32)


def phase_rows(phase, row):
    return pl.ds(32 * row + 16 * (phase >> 1) + (phase & 1), 8, stride=2)


def forward_kernel(step, where, last1, last2, stem, recv, *rest):
    weights, rest = rest[:10], rest[-32:]
    depth1, gains1, inner1, outer1, depth2, gains2, inner2, outer2, down, up = weights
    (
        send, two, one, r2, r1, d2, d1,
        patch, nrm2, act2, coarse, nrm1, act1,
        raw1, raw2, raw_st, st, h1, h2, sh1, sh2, con1, con2,
        v_patch, v_nrm2, v_act2, v_coarse, v_nrm1, v_act1, p2, _, sems,
    ) = rest
    mv = Moves(sems)
    page, spot, first = where[step, 0], where[step, 1], where[step, 2] == 1
    c1, c2 = h1.shape[-1], h2.shape[-1]
    half = c2 // 2
    blocks = c1 // LANES
    c_l1 = [
        mv.bring(last1.at[page, :, LANES * lb : LANES * lb + LANES], raw1.at[lb])
        for lb in range(blocks)
    ]
    c_l2 = mv.bring(last2.at[page], raw2)
    c_st = mv.bring(stem.at[page], raw_st)
    for copy in c_l1:
        copy.wait()
    c_l2.wait()

    @pl.when(first)
    def _():
        for q in range(4):
            for row in range(8):
                for lb in range(blocks):
                    h1[q, 8 * row : 8 * row + 8, LANES * lb : LANES * lb + LANES] = raw1[
                        lb, phase_rows(q, row), :
                    ]
        h2[...] = raw2[...]

    @pl.when(jnp.logical_not(first))
    def _():
        h1[...] = recv[0:4]
        for s in range(2):
            h2[:, half * s : half * s + half] = recv[4 + s]

    low = None
    for q in range(4):
        v_patch[q] = h1[q].astype(BF16)
        part = dot(v_patch[q], down[c1 * q : c1 * q + c1, :])
        low = part if low is None else low + part
    mv.send(v_patch, patch.at[spot])
    two[0] = low
    fill_coarse(sh2, low)
    conv_coarse(sh2, depth2, con2, False)
    unit, scale = normalise(con2[...])
    two[1] = unit
    r2[...] = jnp.broadcast_to(scale, r2.shape)
    v_nrm2[...] = (unit * gains2[0:1, :]).astype(BF16)
    mv.send(v_nrm2, nrm2.at[spot])
    c_st.wait()
    for lb in range(blocks):
        st[lb] = raw_st[:, LANES * lb : LANES * lb + LANES].astype(F32)
    wide2 = inner2.shape[-1]
    for n in range(0, wide2, 512):
        a, s = gelu_pair(dot(v_nrm2[...], inner2[:, n : n + 512]))
        v_act2[:, n : n + 512] = a.astype(BF16)
        d2[:, n : n + 512] = s.astype(BF16)
    mv.send(v_act2, act2.at[spot])
    out2 = dot(v_act2[...], outer2[...])
    two[2] = out2
    prev2 = (h2[...] - gains2[1:2, :] * out2) / gains2[2:3, :]
    for s in range(2):
        send[4 + s] = prev2[:, half * s : half * s + half]
    v_coarse[...] = prev2.astype(BF16)
    mv.send(v_coarse, coarse.at[spot])
    p2[...] = dot(v_coarse[...], up[...])
    for q in range(4):
        for row in range(8):
            at = slice(8 * row, 8 * row + 8)
            for lb in range(blocks):
                lanes = slice(LANES * lb, LANES * lb + LANES)
                one[0, q, at, lanes] = st[lb, phase_rows(q, row), :] + p2[at, lanes]
        fill_fine(sh1, one[0, q], q)
    conv_fine(sh1, depth1, con1, False)
    for q in range(4):
        unit, scale = normalise(con1[q])
        one[1, q] = unit
        r1[q] = jnp.broadcast_to(scale, r1.shape[1:])
        v_nrm1[64 * q : 64 * q + 64, :] = (unit * gains1[0:1, :]).astype(BF16)
    mv.send(v_nrm1, nrm1.at[spot])
    wide1 = inner1.shape[-1]
    for n in range(0, wide1, 256):
        a, s = gelu_pair(dot(v_nrm1[...], inner1[:, n : n + 256]))
        v_act1[:, n : n + 256] = a.astype(BF16)
        d1[:, n : n + 256] = s.astype(BF16)
    mv.send(v_act1, act1.at[spot])
    for q in range(4):
        out1 = dot(v_act1[64 * q : 64 * q + 64, :], outer1[...])
        one[2, q] = out1
        send[q] = (h1[q] - gains1[1:2, :] * out1) / gains1[2:3, :]
    mv.finish()


def backward_kernel(step, where, last1, last2, teach1, teach2, recv, prev, *rest):
    two, one, r2, r1, d2, d1 = rest[:6]
    depth1, gains1, inner1, outer1, depth2, gains2, inner2, outer2, down, up = rest[6:16]
    (
        send, gout2, gpre2, glow, gout1, gpre1, gpool, stem, small,
        raw1, raw2, te1, te2, tf1, g1, g2, sh1, sh2, low_g, ent_g,
        v_gout2, v_gpre2, v_glow, v_gout1, v_gpre1, v_gpool, v_small, v_stem,
        sems,
    ) = rest[-29:]
    mv = Moves(sems)
    page, spot, first, slot = where[step, 0], where[step, 1], where[step, 2] == 1, where[step, 3]
    c1, c2 = g1.shape[-1], g2.shape[-1]
    half = c2 // 2
    blocks = c1 // LANES
    c_in = [
        mv.bring(last1.at[page, :, LANES * lb : LANES * lb + LANES], raw1.at[lb])
        for lb in range(blocks)
    ]
    c_in.append(mv.bring(last2.at[page], raw2))
    c_in.append(mv.bring(teach1.at[slot], te1))
    c_in.append(mv.bring(teach2.at[slot], te2))
    v_small[...] = jnp.zeros_like(v_small)
    for copy in c_in:
        copy.wait()

    @pl.when(first)
    def _():
        g2[...] = (raw2[...] - te2[...].astype(F32)) / 8.0
        for lb in range(blocks):
            tf1[lb] = te1[:, LANES * lb : LANES * lb + LANES].astype(F32)
        for q in range(4):
            for row in range(8):
                at, rows = slice(8 * row, 8 * row + 8), phase_rows(q, row)
                for lb in range(blocks):
                    g1[q, at, LANES * lb : LANES * lb + LANES] = (
                        raw1[lb, rows, :] - tf1[lb, rows, :]
                    ) / 16.0

    @pl.when(jnp.logical_not(first))
    def _():
        g1[...] = recv[0:4]
        for s in range(2):
            g2[:, half * s : half * s + half] = recv[4 + s]

    v_gout2[...] = (gains2[1:2, :] * g2[...]).astype(BF16)
    mv.send(v_gout2, gout2.at[spot])
    wide2 = inner2.shape[-1]
    for n in range(0, wide2, 512):
        part = dot_nt(v_gout2[...], outer2[n : n + 512, :])
        v_gpre2[:, n : n + 512] = (part * d2[:, n : n + 512].astype(F32)).astype(BF16)
    mv.send(v_gpre2, gpre2.at[spot])
    gn = dot_nt(v_gpre2[...], inner2[...])
    unit = two[1]
    v_small[56:57, :] = jnp.sum(gn * unit, axis=0, keepdims=True)
    v_small[57:58, :] = jnp.sum(g2[...] * two[2], axis=0, keepdims=True)
    for s in range(2):
        lanes = slice(half * s, half * s + half)
        v_small[58:59, lanes] = jnp.sum(g2[:, lanes] * prev[4 + s], axis=0, keepdims=True)
    fill_coarse(sh2, norm_back(gn, unit, r2[:, 0:1], gains2[0:1, :]))
    conv_coarse(sh2, depth2, low_g, True)
    v_glow[...] = low_g[...].astype(BF16)
    mv.send(v_glow, glow.at[spot])
    gamma = jnp.zeros((1, c1), F32)
    layer = jnp.zeros((1, c1), F32)
    for q in range(4):
        total = g1[q] + dot_nt(v_glow[...], down[c1 * q : c1 * q + c1, :])
        gamma += jnp.sum(total * prev[q], axis=0, keepdims=True)
        layer += jnp.sum(total * one[2, q], axis=0, keepdims=True)
        v_gout1[64 * q : 64 * q + 64, :] = (gains1[1:2, :] * total).astype(BF16)
        send[q] = gains1[2:3, :] * total
    mv.send(v_gout1, gout1.at[spot])
    taps_coarse(sh2, two.at[0], v_small.at[0:56])
    wide1 = inner1.shape[-1]
    for n in range(0, wide1, 256):
        part = dot_nt(v_gout1[...], outer1[n : n + 256, :])
        v_gpre1[:, n : n + 256] = (part * d1[:, n : n + 256].astype(F32)).astype(BF16)
    mv.send(v_gpre1, gpre1.at[spot])
    ggain = jnp.zeros((1, c1), F32)
    for q in range(4):
        gn = dot_nt(v_gpre1[64 * q : 64 * q + 64, :], inner1[...])
        unit = one[1, q]
        ggain += jnp.sum(gn * unit, axis=0, keepdims=True)
        fill_fine(sh1, norm_back(gn, unit, r1[q, :, 0:1], gains1[0:1, :]), q)
    v_small[120:121, 0:c1] = ggain
    v_small[121:122, 0:c1] = layer
    v_small[122:123, 0:c1] = gamma
    conv_fine(sh1, depth1, ent_g, True)
    for q in range(4):
        for row in range(8):
            for lb in range(blocks):
                v_stem[lb, phase_rows(q, row), :] = ent_g[
                    q, 8 * row : 8 * row + 8, LANES * lb : LANES * lb + LANES
                ]
    for lb in range(blocks):
        mv.send(v_stem.at[lb], stem.at[spot, :, LANES * lb : LANES * lb + LANES])
    v_gpool[...] = (ent_g[0] + ent_g[1] + ent_g[2] + ent_g[3]).astype(BF16)
    mv.send(v_gpool, gpool.at[spot])
    next2 = gains2[2:3, :] * g2[...] + dot_nt(v_gpool[...], up[...])
    for s in range(2):
        send[4 + s] = next2[:, half * s : half * s + half]
    taps_fine(sh1, one.at[0], v_small.at[64:120, 0:c1])
    mv.send(v_small, small.at[spot])
    mv.finish()


ANY = pl.BlockSpec(memory_space=pl.ANY)
SMEM = pl.BlockSpec(memory_space=pltpu.SMEM)
INSIDE = pl.BlockSpec(memory_space=pltpu.VMEM)
VMEM_LIMIT = PAGE_VMEM = 20 * 1024 * 1024


def sds(shape, dtype):
    return jax.ShapeDtypeStruct(tuple(shape), dtype)


def page_sizes(weights):
    depth1, gains1, inner1, outer1, depth2, gains2, inner2, outer2, down, up = weights
    return gains1.shape[-1], gains2.shape[-1], inner1.shape[-1], inner2.shape[-1]


def forward_call(step, where, fields, recv, weights, kept, stacks):
    c1, c2, e1, e2 = page_sizes(weights)
    last1, last2, stem = fields
    temps = [
        sds(recv.shape, F32), sds((3, 64, c2), F32), sds((3, 4, 64, c1), F32),
        sds((64, LANES), F32), sds((4, 64, LANES), F32), sds((64, e2), BF16), sds((256, e1), BF16),
    ]
    out_shape = temps + list(kept)
    in_specs = [SMEM] + [ANY] * 3 + [INSIDE] * (1 + len(weights)) + [ANY] * len(stacks)
    first_stack = 5 + len(weights)
    blocks = c1 // LANES
    scratch = [
        pltpu.VMEM((blocks, 256, LANES), F32), pltpu.VMEM((64, c2), F32),
        pltpu.VMEM((256, c1), BF16), pltpu.VMEM((blocks, 256, LANES), F32),
        pltpu.VMEM((4, 64, c1), F32), pltpu.VMEM((64, c2), F32),
        pltpu.VMEM((4, 4, 64, c1), F32), pltpu.VMEM((7, 64, c2), F32),
        pltpu.VMEM((4, 64, c1), F32), pltpu.VMEM((64, c2), F32),
    ]
    scratch += [pltpu.VMEM(s.shape[1:], s.dtype) for s in kept]
    scratch += [pltpu.VMEM((64, c1), F32), pltpu.VMEM((8, LANES), F32)]
    scratch += [pltpu.SemaphoreType.DMA((24,))]
    macs = 64 * (4 * c1 * c2 + 2 * c2 * e2 + c2 * c1) + 256 * 2 * c1 * e1
    outs = pl.pallas_call(
        functools.partial(forward_kernel, step),
        out_shape=out_shape,
        in_specs=in_specs,
        out_specs=[INSIDE] * len(temps) + [ANY] * len(kept),
        scratch_shapes=scratch,
        input_output_aliases={first_stack + k: len(temps) + k for k in range(len(stacks))},
        compiler_params=pltpu.CompilerParams(vmem_limit_bytes=PAGE_VMEM),
        cost_estimate=pl.CostEstimate(flops=2 * macs, bytes_accessed=20 << 20, transcendentals=0),
        name="forward_page",
    )(where, last1, last2, stem, recv, *weights, *stacks)
    return outs[0], outs[1 : len(temps)], tuple(outs[len(temps) :])


def backward_call(step, where, fields, recv, prev, temps, weights, kept, stacks):
    c1, c2, e1, e2 = page_sizes(weights)
    last1, last2, teach1, teach2 = fields
    out_shape = [sds(recv.shape, F32)] + list(kept)
    inside = 2 + len(temps) + len(weights)
    in_specs = [SMEM] + [ANY] * 4 + [INSIDE] * inside + [ANY] * len(stacks)
    first_stack = 5 + inside
    blocks = c1 // LANES
    scratch = [
        pltpu.VMEM((blocks, 256, LANES), F32), pltpu.VMEM((64, c2), F32),
        pltpu.VMEM((256, c1), BF16), pltpu.VMEM((64, c2), BF16),
        pltpu.VMEM((blocks, 256, LANES), F32),
        pltpu.VMEM((4, 64, c1), F32), pltpu.VMEM((64, c2), F32),
        pltpu.VMEM((4, 4, 64, c1), F32), pltpu.VMEM((7, 64, c2), F32),
        pltpu.VMEM((64, c2), F32), pltpu.VMEM((4, 64, c1), F32),
    ]
    held = [pltpu.VMEM(s.shape[1:], s.dtype) for s in kept]
    scratch += held[:6] + held[7:]
    scratch += [pltpu.VMEM((blocks, 256, LANES), F32), pltpu.SemaphoreType.DMA((24,))]
    macs = 64 * (4 * c1 * c2 + 2 * c2 * e2 + c2 * c1) + 256 * 2 * c1 * e1
    outs = pl.pallas_call(
        functools.partial(backward_kernel, step),
        out_shape=out_shape,
        in_specs=in_specs,
        out_specs=[INSIDE] + [ANY] * len(kept),
        scratch_shapes=scratch,
        input_output_aliases={first_stack + k: 1 + k for k in range(len(stacks))},
        compiler_params=pltpu.CompilerParams(vmem_limit_bytes=PAGE_VMEM),
        cost_estimate=pl.CostEstimate(flops=2 * macs, bytes_accessed=20 << 20, transcendentals=0),
        name="backward_page",
    )(where, last1, last2, teach1, teach2, recv, prev, *temps, *weights, *stacks)
    return outs[0], tuple(outs[1:])


def kept_shapes(pages, c1, c2, e1, e2):
    n = pages + 1
    ahead = (
        sds((n, 4, 64, c1), BF16), sds((n, 64, c2), BF16), sds((n, 64, e2), BF16),
        sds((n, 64, c2), BF16), sds((n, 256, c1), BF16), sds((n, 256, e1), BF16),
    )
    back = (
        sds((n, 64, c2), BF16), sds((n, 64, e2), BF16), sds((n, 64, c2), BF16),
        sds((n, 256, c1), BF16), sds((n, 256, e1), BF16), sds((n, 64, c1), BF16),
        sds((n, 256, c1), F32), sds((n, 128, c2), F32),
    )
    return ahead, back


def plan(c1, c2, e1, e2, pieces):
    whole = (e2 // 2, c2 * e2 // (2 * c2), 2 * c1, c1 * e1 // (2 * c2), c1 * e1 // (2 * c2), c1 // 2)
    rows = [n // pieces for n in whole] + [8]
    starts = [sum(rows[:k]) for k in range(len(rows) + 1)]
    return rows, starts


def piece_index(bits, masks_count, group, rel):
    index = jnp.int32(group)
    for s in range(masks_count):
        own = bits[s if group == 0 else masks_count - 1 - s]
        index = 2 * index + (own + rel[s]) % 2
    return index


def rel_bits(value, count):
    return tuple((value >> (count - 1 - s)) & 1 for s in range(count))


def weight_kernel(levels, pages, sizes, where, *refs):
    c1, c2, e1, e2 = sizes
    pieces = 2 << levels
    rows, starts = plan(c1, c2, e1, e2, pieces)
    (
        patch, nrm2, act2, coarse, nrm1, act1, gout2, gpre2, glow, gout1, gpre1, gpool, small,
        first, later,
        v_patch, v_nrm2, v_act2, v_coarse, v_nrm1, v_act1,
        v_gout2, v_gpre2, v_glow, v_gout1, v_gpre1, v_gpool, v_small, flat, sems,
    ) = refs
    mv = Moves(sems)
    half = where[0]
    bits = [where[1 + s] for s in range(levels)]

    def part(ref, width):
        return ref.at[0:pages, :, pl.ds(pl.multiple_of(half * width, width), width)]

    w_act1 = mv.bring(part(act1, e1 // 2), v_act1)
    w_gout1 = mv.bring(gout1.at[0:pages], v_gout1)
    w_nrm1 = mv.bring(nrm1.at[0:pages], v_nrm1)
    w_gpre1 = mv.bring(part(gpre1, e1 // 2), v_gpre1)
    w_act2 = mv.bring(part(act2, e2 // 2), v_act2)
    w_gout2 = mv.bring(gout2.at[0:pages], v_gout2)
    w_nrm2 = mv.bring(nrm2.at[0:pages], v_nrm2)
    w_gpre2 = mv.bring(part(gpre2, e2 // 2), v_gpre2)
    w_patch = mv.bring(patch.at[0:pages, pl.ds(2 * half, 2)], v_patch)
    w_glow = mv.bring(glow.at[0:pages], v_glow)
    w_coarse = mv.bring(part(coarse, c2 // 2), v_coarse)
    w_gpool = mv.bring(gpool.at[0:pages], v_gpool)
    w_small = mv.bring(small.at[0:pages, pl.ds(pl.multiple_of(64 * half, 64), 64)], v_small)

    def flatten(value):
        return value.reshape(-1, value.shape[-1])

    def product(left, right):
        return lax.dot_general(left, right, (((0,), (0,)), ((), ())), preferred_element_type=F32)

    def place(section, row, value, lane=0):
        size = rows[section]
        done = 0
        while done < value.shape[0]:
            p, inside = divmod(row + done, size)
            count = min(size - inside, value.shape[0] - done)
            at = starts[section] + inside
            flat[p, at : at + count, lane : lane + value.shape[1]] = value[done : done + count]
            done += count

    w_act1.wait()
    w_gout1.wait()
    right = flatten(v_gout1[...])
    lanes = c2 // c1
    run = e1 // 2 // lanes
    for k in range(lanes):
        place(4, 0, product(flatten(v_act1[:, :, run * k : run * k + run]), right), c1 * k)
    w_nrm1.wait()
    w_gpre1.wait()
    left = flatten(v_nrm1[...])
    for k in range(e1 // 2 // c2):
        place(3, c1 * k, product(left, flatten(v_gpre1[:, :, c2 * k : c2 * k + c2])))
    w_act2.wait()
    w_gout2.wait()
    right = flatten(v_gout2[...])
    for r in range(0, e2 // 2, 256):
        place(0, r, product(flatten(v_act2[:, :, r : r + 256]), right))
    w_nrm2.wait()
    w_gpre2.wait()
    for k in range(e2 // 2 // c2):
        right = flatten(v_gpre2[:, :, c2 * k : c2 * k + c2])
        for r in range(0, c2, 256):
            place(1, c2 * k + r, product(flatten(v_nrm2[:, :, r : r + 256]), right))
    w_patch.wait()
    w_glow.wait()
    right = flatten(v_glow[...])
    for q in range(2):
        place(2, c1 * q, product(flatten(v_patch[:, q]), right))
    w_coarse.wait()
    w_gpool.wait()
    right = flatten(v_gpool[...])
    run = c2 // 2 // lanes
    for k in range(lanes):
        place(5, 0, product(flatten(v_coarse[:, :, run * k : run * k + run]), right), c1 * k)
    w_small.wait()
    total = v_small[0]
    for p in range(1, pages):
        total = total + v_small[p]
    for p in range(min(pieces, total.shape[0] // 8)):
        flat[p, starts[6] : starts[7], :] = total[8 * p : 8 * p + 8]
    for p in range(total.shape[0] // 8, pieces):
        flat[p, starts[6] : starts[7], :] = jnp.zeros((8, c2), F32)
    slot = 0
    each = pieces // 4
    for group in range(2):
        for value in range(2 * each):
            rel = rel_bits(value, levels)
            index = piece_index(bits, levels, group, rel)
            out = first if rel[0] == 1 else later
            mv.send(flat.at[index], out.at[each * group + value % each])
    mv.finish()


def weight_call(where, levels, pages, sizes, arrays):
    c1, c2, e1, e2 = sizes
    pieces = 2 << levels
    rows, starts = plan(c1, c2, e1, e2, pieces)
    scratch = [
        pltpu.VMEM((pages, 2, 64, c1), BF16), pltpu.VMEM((pages, 64, c2), BF16),
        pltpu.VMEM((pages, 64, e2 // 2), BF16), pltpu.VMEM((pages, 64, c2 // 2), BF16),
        pltpu.VMEM((pages, 256, c1), BF16), pltpu.VMEM((pages, 256, e1 // 2), BF16),
        pltpu.VMEM((pages, 64, c2), BF16), pltpu.VMEM((pages, 64, e2 // 2), BF16),
        pltpu.VMEM((pages, 64, c2), BF16), pltpu.VMEM((pages, 256, c1), BF16),
        pltpu.VMEM((pages, 256, e1 // 2), BF16), pltpu.VMEM((pages, 64, c1), BF16),
        pltpu.VMEM((pages, 64, c2), F32), pltpu.VMEM((pieces, starts[7], c2), F32),
        pltpu.SemaphoreType.DMA((16 + pieces,)),
    ]
    out = sds((pieces // 2, starts[7], c2), F32)
    macs = pages * (64 * (c1 * 4 * c2 + 2 * c2 * e2 + c2 * c1) + 256 * 2 * c1 * e1) // 2

    def kernel(*refs):
        weight_kernel(levels, pages, sizes, *refs)

    return pl.pallas_call(
        kernel,
        out_shape=[out, out],
        in_specs=[SMEM] + [ANY] * len(arrays),
        out_specs=[ANY, ANY],
        scratch_shapes=scratch,
        compiler_params=pltpu.CompilerParams(vmem_limit_bytes=VMEM_LIMIT),
        cost_estimate=pl.CostEstimate(flops=2 * macs, bytes_accessed=14 << 20, transcendentals=0),
        name="weight_half",
    )(where, *arrays)


def spread_kernel(levels, sizes, keys, where, *refs):
    c1, c2, e1, e2 = sizes
    pieces = 2 << levels
    rows, starts = plan(c1, c2, e1, e2, pieces)
    n = len(keys)
    parts = refs[:n]
    in1, out1, in2, out2, down, up, k1, s1, k2, s2, landed, sems, back, tail = refs[-14:]
    bits = [where[1 + s] for s in range(levels)]
    lanes = c2 // c1
    for k in range(n):
        pltpu.make_async_copy(parts[k], landed.at[k], sems.at[k]).start()
    waits = []
    for k, (core, group, rel) in enumerate(keys):
        pltpu.make_async_copy(parts[k], landed.at[k], sems.at[k]).wait()
        half = (where[0] + core) % 2
        p = piece_index(bits, levels, group, rel)
        src, sem = landed.at[k], back.at[k]

        def go(section, dst, lane=None, src=src, sem=sem):
            piece = src.at[starts[section] : starts[section + 1]]
            if lane is not None:
                piece = piece.at[:, c1 * lane : c1 * lane + c1]
            pltpu.make_async_copy(piece, dst, sem).start()

        def span(base, count):
            return pl.ds(pl.multiple_of(base, count), count)

        go(0, out2.at[span(half * (e2 // 2) + rows[0] * p, rows[0]), :])
        per = c2 // rows[1]
        go(1, in2.at[
            span((p % per) * rows[1], rows[1]),
            span(half * (e2 // 2) + c2 * (p // per), c2),
        ])
        go(2, down.at[span(half * (2 * c1) + rows[2] * p, rows[2]), :])
        go(3, in1.at[span(rows[3] * p, rows[3]), span(half * (e1 // 2), c2)])
        for k2_ in range(lanes):
            run = e1 // 2 // lanes
            go(4, out1.at[span(half * (e1 // 2) + run * k2_ + rows[4] * p, rows[4]), :], k2_)
            run = c2 // 2 // lanes
            go(5, up.at[span(half * (c2 // 2) + run * k2_ + rows[5] * p, rows[5]), :], k2_)
        tail[span(pieces * 8 * half + 8 * p, 8), :] = landed[k, starts[6] : starts[7], :]
        sent = landed.at[k, 0 : starts[6]]
        waits.append(pltpu.make_async_copy(sent, sent, sem))
    for copy in waits:
        copy.wait()
    base = [0, pieces * 8]
    k2[...] = tail[0:49, :]
    s2[...] = tail[56:64, :]
    k1[...] = tail[base[1] : base[1] + 49, 0:c1]
    s1[...] = tail[base[1] + 56 : base[1] + 64, 0:c1]


def spread_call(where, levels, sizes, table):
    c1, c2, e1, e2 = sizes
    pieces = 2 << levels
    starts = plan(c1, c2, e1, e2, pieces)[1]
    keys = sorted(table)
    parts = [table[k] for k in keys]
    outs = [
        sds((c1, e1), F32), sds((e1, c1), F32), sds((c2, e2), F32), sds((e2, c2), F32),
        sds((4 * c1, c2), F32), sds((c2, c1), F32),
        sds((49, c1), F32), sds((8, c1), F32), sds((49, c2), F32), sds((8, c2), F32),
    ]

    def kernel(*refs):
        spread_kernel(levels, sizes, keys, *refs)

    return pl.pallas_call(
        kernel,
        out_shape=outs,
        in_specs=[SMEM] + [ANY] * len(parts),
        out_specs=[ANY] * 6 + [INSIDE] * 4,
        scratch_shapes=[
            pltpu.VMEM((len(parts), starts[7], c2), F32),
            pltpu.SemaphoreType.DMA((len(parts),)), pltpu.SemaphoreType.DMA((len(parts),)),
            pltpu.VMEM((16 * pieces, c2), F32),
        ],
        compiler_params=pltpu.CompilerParams(vmem_limit_bytes=VMEM_LIMIT),
        cost_estimate=pl.CostEstimate(flops=0, bytes_accessed=26 << 20, transcendentals=0),
        name="spread",
    )(where, *parts)


def swap(value, mask):
    return lax.ppermute(value, "dp", [(i, i ^ mask) for i in range(lax.axis_size("dp"))])


def device_bits():
    levels = lax.axis_size("dp").bit_length() - 2
    index = lax.axis_index("dp")
    core = index & 1
    bits = [(index >> (s + 1)) & 1 for s in range(levels)]
    return (
        jnp.stack([core] + bits).astype(jnp.int32),
        jnp.stack([1 - core] + bits).astype(jnp.int32),
    )


def sum_all(arrays, field, pages, sizes, where, other):
    levels = lax.axis_size("dp").bit_length() - 2
    columns = lax.axis_size("col")
    masks = [2 << s for s in range(levels)]
    order = [masks, masks[::-1]]
    lower = [(i, i - 1) for i in range(1, columns)]
    upper = [(i - 1, i) for i in range(1, columns)]
    hops = {"left": columns - 1, "down": field, "up": field}

    def hop():
        hops["left"] -= 1
        down, up = (lax.ppermute(hops[k], "col", r) for k, r in (("down", lower), ("up", upper)))
        if hops["left"]:
            down, up = field + down, field + up
        return down, up

    def together(values, moved):
        if moved is None:
            return values
        keys = list(values)
        out = lax.optimization_barrier((moved, [values[k] for k in keys]))
        hops["down"], hops["up"] = out[0]
        return dict(zip(keys, out[1]))

    their_first, their_later = weight_call(other, levels, pages, sizes, arrays)
    got_first = swap(their_first, 1)
    my_first, my_later = weight_call(where, levels, pages, sizes, arrays)
    got_later = swap(their_later, 1)
    each = 1 << (levels - 1)
    held = {}
    for group in range(2):
        for value in range(2 * each):
            rel = rel_bits(value, levels)
            mine, got = (my_first, got_first) if rel[0] else (my_later, got_later)
            k = each * group + value % each
            held[group, rel] = mine[k] + got[k]
    moved = hop() if hops["left"] else None
    for s in range(levels):
        for value in reversed(range(1 << (levels - 1 - s))):
            for group in range(2):
                rest = rel_bits(value, levels - 1 - s)
                there, here = (0,) * s + (1,) + rest, (0,) * (s + 1) + rest
                arrived = swap(held.pop((group, there)), order[group][s])
                held[group, here] = held[group, here] + arrived
        if s == 0:
            held = together(held, moved)
            moved = hop() if hops["left"] else None
    table = {}

    def keep(group, rel, value):
        table[0, group, rel] = value
        table[1, group, rel] = swap(value, 1)

    for group in range(2):
        keep(group, (0,) * levels, held[group, (0,) * levels])
    for s in reversed(range(levels)):
        if s == 0:
            table = together(table, moved)
            while hops["left"]:
                hops["down"], hops["up"] = hop()
        for value in range(1 << (levels - 1 - s)):
            for group in range(2):
                rest = rel_bits(value, levels - 1 - s)
                here, there = (0,) * (s + 1) + rest, (0,) * s + (1,) + rest
                keep(group, there, swap(table[0, group, here], order[group][s]))
    total = field + hops["down"] + hops["up"] if columns > 1 else field
    return spread_call(where, levels, sizes, table), total


def local(
    stem_map, last_one, last_two, teach_one, teach_two, teacher_slot,
    depth_one, gains_one, inner_one, outer_one, depth_two, gains_two, inner_two, outer_two,
    down_proj, up_proj,
):
    columns = lax.axis_size("col")
    position = lax.axis_index("col")
    pages = stem_map.shape[0]
    c1, c2 = last_one.shape[-1], last_two.shape[-1]
    sizes = (c1, c2, inner_one.shape[-1], inner_two.shape[-1])
    last1 = last_one.reshape(pages, 256, c1)
    last2 = last_two.reshape(pages, 64, c2)
    stem = stem_map.reshape(pages, 256, c1)
    teach1 = teach_one.reshape(pages, 256, c1)
    teach2 = teach_two.reshape(pages, 64, c2)
    weights = (
        depth_one[0].astype(F32), gains_one[0], inner_one[0], outer_one[0],
        depth_two[0].astype(F32), gains_two[0], inner_two[0], outer_two[0],
        down_proj[0], up_proj[0],
    )
    first = (position == columns - 1).astype(jnp.int32)
    route = [(i, i - 1) for i in range(1, columns)]
    ahead_shapes, back_shapes = kept_shapes(pages, *sizes)
    blank = jnp.zeros((6, 64, c1), F32)

    steps = columns + pages - 1
    micro = jnp.arange(steps, dtype=jnp.int32) - (columns - 1 - position)
    active = jnp.logical_and(micro >= 0, micro < pages)
    page = jnp.clip(micro, 0, pages - 1)
    where = jnp.stack(
        [page, jnp.where(active, micro, pages), jnp.full_like(page, first), teacher_slot[page]],
        axis=1,
    ).astype(jnp.int32)
    where, mine, other = lax.optimization_barrier((where,) + device_bits())
    recv_high = recv_grad = blank
    ahead = back = ()
    for k in range(steps):
        prev, temps, ahead = forward_call(
            k, where, (last1, last2, stem), recv_high, weights, ahead_shapes, ahead
        )
        if k < steps - 1:
            recv_high = lax.ppermute(prev, "col", route)
        out_grad, back = backward_call(
            k, where, (last1, last2, teach1, teach2), recv_grad, prev, temps, weights,
            back_shapes, back,
        )
        if k < steps - 1:
            recv_grad = lax.ppermute(out_grad, "col", route)
    grads, stem_total = sum_all(
        ahead + back[:6] + back[7:], back[6][:pages], pages, sizes, mine, other
    )
    in1, out1, in2, out2, down, up, k1, s1, k2, s2 = grads
    stem_total = stem_total.reshape(stem_map.shape)
    return (
        k1[None], s1[None, :3], in1[None], out1[None], k2[None], s2[None, :2], s2[2:3],
        in2[None], out2[None], down[None], up[None], stem_total,
    )


def solution(mesh):
    paged, row, mat = P("dp", None, None, None), P("col", None), P("col", None, None)
    return jax.shard_map(
        local,
        mesh=mesh,
        in_specs=(paged,) * 5 + (P("dp"),) + (mat,) * 10,
        out_specs=(mat,) * 6 + (row,) + (mat,) * 4 + (paged,),
        check_vma=False,
    )
```
